256 devices in a mesh: pairs: 32 (over x, y, core), coef: 8 (over z).
Axes of the slice: x: 4, y: 4, z: 8, core: 2. Of those that a mesh axis runs over, the one named last changes fastest.
Arguments:
- integrals: bfloat16 [4096, 64, 64, 64], P('pairs', 'coef'), may hold values from -6 to 6
- block_shells: int32 [32, 64, 2], P('pairs', 'coef'), may hold values from 0 to 143
- live_counts: int32 [32, 8], P('pairs', 'coef'), may hold values from 1 to 8, as said below
- significance: int32 [144, 144], replicated, may hold values 0 or 1
- occ_coef: bfloat16 [9216, 64], P('coef'), may hold values from -0.375 to 0.375
- lam_coef: bfloat16 [64, 128], P('coef'), may hold values from -0.75 to 0.75
- sig_coef: bfloat16 [64, 128], P('coef'), may hold values from -0.75 to 0.75
Outputs:
- mo_integrals: float32 [4096, 128, 128], P(('pairs', 'coef'))
The draws below stay inside these ranges and needn't reach their ends.
Inputs may be any that keep to these rules, and one draw needn't show every extreme that they name: `live_counts`: each device's live slots are its first ones; some device has all 8 live.
All inputs are finite; a program needn't handle non-finite values.
Results may differ from the reference program's by a relative error of at most 0.0029.
Values may be sent and summed in bfloat16 or wider, within the bound.
No kernel may reach another device: no remote copies, remote signals or barrier semaphores. Data moves between devices by JAX's collectives and lax.ppermute only.
A program may use at most 64 MiB of HBM per device.

```python
import jax
import jax.numpy as jnp
from jax import lax

SHELL = 64
NSH = 144
OCC = 64
LAMW = 64
SIGW = 64
VIRT = 128
NBLK = 8
NBF = 9216
LS = 4096
N_PAIRS = 32
N_COEF = 8


def draw_live_counts(key, part):
    key = jax.random.fold_in(key, 11)
    first_key, second_key = jax.random.split(key)
    total = N_PAIRS * N_COEF
    values = jax.random.randint(first_key, (total,), 1, NBLK + 1)
    chosen = jax.random.randint(second_key, (), 0, total)
    values = jnp.where(jnp.arange(total) == chosen, NBLK, values)
    return values.reshape(N_PAIRS, N_COEF).astype(jnp.int32)


def with_ends(drawn, stream_key, least, top_value):
    dims = drawn.shape
    spot = [jax.random.randint(jax.random.fold_in(stream_key, axis), (), 0, dims[axis]) for axis in range(len(dims))]
    drawn = drawn.at[tuple(spot)].set(least)
    longest = dims.index(max(dims))
    spot[longest] = (spot[longest] + 1) % dims[longest]
    return drawn.at[tuple(spot)].set(top_value)


def levels(rng, shape, pieces, smallest, top_value):
    def one(dim, blocks):
        steps = jax.random.uniform(jax.random.fold_in(jax.random.fold_in(rng, 6), dim), (blocks,), jnp.float32, smallest / len(pieces), top_value / len(pieces))
        return jnp.repeat(jnp.exp(steps), shape[dim] // blocks).reshape((-1,) + (1,) * (len(shape) - dim - 1))

    factor_of = one(*pieces[0])
    for cut in pieces[1:]:
        factor_of = factor_of * one(*cut)
    return factor_of


def centred(rng, shape, scale, bound, cuts=(), kind=jnp.bfloat16):
    loudness = levels(rng, shape, cuts, -0.22, 0.18) if cuts else 1.0
    entries = jax.random.normal(rng, shape, jnp.float32) * scale * loudness
    return jnp.minimum(jnp.maximum(entries, -bound), bound).astype(kind)


def setup_inputs(seed: int = 0) -> dict:
    key_list = jax.random.split(jax.random.key(seed), 8)
    integrals = centred(key_list[0], (LS, NBLK * N_COEF, SHELL, SHELL), 1.0, 6.0, ((0, 32), (1, 8)))
    block_shells = with_ends(jax.random.randint(key_list[1], (N_PAIRS, NBLK * N_COEF, 2), 0, NSH), jax.random.fold_in(key_list[1], 1), 0, NSH - 1).astype(jnp.int32)
    live_counts = draw_live_counts(jax.random.fold_in(key_list[7], 71), 0)
    significance = with_ends((jax.random.randint(key_list[3], (NSH, NSH), 0, 4) < 3).astype(jnp.int32), jax.random.fold_in(key_list[3], 1), 0, 1)
    occ_coef = centred(key_list[4], (NBF, OCC), 256 ** -0.5, 0.375, ((0, 8),))
    lam_coef = centred(key_list[5], (LAMW, VIRT), LAMW ** -0.5, 0.75, ((0, 8),))
    sig_coef = centred(key_list[6], (SIGW, VIRT), SIGW ** -0.5, 0.75, ((0, 8),))
    return {"integrals": integrals, "block_shells": block_shells, "live_counts": live_counts, "significance": significance, "occ_coef": occ_coef, "lam_coef": lam_coef, "sig_coef": sig_coef}


def reference(integrals, block_shells, live_counts, significance, occ_coef, lam_coef, sig_coef):
    slots_all = integrals.shape[1]
    per_device = slots_all // N_COEF
    shell_table = occ_coef.reshape(NSH, SHELL, OCC)
    grouped = integrals.reshape(N_PAIRS, LS // N_PAIRS, slots_all, SHELL, SHELL)

    def one_group(packed):
        tiles, shells_here, counts_here = packed
        rows = shell_table[shells_here[:, 0]].astype(jnp.float32)
        cols = shell_table[shells_here[:, 1]].astype(jnp.float32)
        screened = significance[shells_here[:, 0], shells_here[:, 1]]
        slot = jnp.arange(slots_all, dtype=jnp.int32)
        limit = counts_here[slot // per_device]
        live = ((slot % per_device) < limit) & (screened == 1)
        quarter = jnp.einsum("smi,lsmn->lsin", rows, tiles.astype(jnp.float32)).astype(jnp.bfloat16)
        weighted = cols * live.astype(jnp.float32)[:, None, None]
        return jnp.einsum("lsin,snj->lij", quarter.astype(jnp.float32), weighted)

    halves = lax.map(one_group, (grouped, block_shells, live_counts))
    pair_tensor = halves.reshape(LAMW, SIGW, OCC * OCC)
    partly = jnp.einsum("xa,xyq->qay", lam_coef.astype(jnp.float32), pair_tensor, precision=lax.Precision.HIGHEST)
    return jnp.einsum("qay,yb->qab", partly, sig_coef.astype(jnp.float32), precision=lax.Precision.HIGHEST)
```

```python
import jax
import jax.numpy as jnp
from jax import lax
from jax.sharding import PartitionSpec as P


def on_device(integrals, block_shells, live_counts, significance, occ_coef, lam_coef, sig_coef):
    core = lax.axis_index("pairs") % 2
    n_coef = lax.axis_size("coef")
    n_pairs = lax.axis_size("pairs")
    mine = lax.dynamic_slice_in_dim(occ_coef.T, core * 32, 32, axis=0)
    mine = mine.reshape(32, 9, 128).transpose(1, 0, 2).reshape(288, 128)
    panel = jnp.where(core == 0, lam_coef, sig_coef)
    mine = jnp.concatenate([mine, panel], axis=0)
    copies = jnp.broadcast_to(mine[None], (n_coef,) + mine.shape)
    got = lax.all_to_all(copies, "coef", 0, 0, tiled=True)
    other = lax.ppermute(got, "pairs", [(i, i ^ 1) for i in range(n_pairs)])
    low = jnp.where(core == 0, got, other)
    high = jnp.where(core == 0, other, got)
    lam_panel = low[:, 288:].reshape(64, 128)
    sig_panel = high[:, 288:].reshape(64, 128)
    table = jnp.stack([low[:, :288].reshape(72, 32, 128), high[:, :288].reshape(72, 32, 128)], axis=1)
    table = table.reshape(72, 64, 2, 64).transpose(0, 2, 1, 3).reshape(144, 64, 64)

    pair_shells = block_shells[0]
    row_shells = table[pair_shells[:, 0]]
    col_shells = table[pair_shells[:, 1]]
    screened = significance[pair_shells[:, 0], pair_shells[:, 1]]
    is_live = (jnp.arange(8) < live_counts[0, 0]) & (screened == 1)
    col_weighted = col_shells * is_live.astype(jnp.bfloat16)[:, None, None]
    quarter = jnp.einsum(
        "sim,lsmn->lsin", row_shells, integrals, preferred_element_type=jnp.float32
    ).astype(jnp.bfloat16)
    half = jnp.einsum(
        "lsin,sjn->ijl", quarter, col_weighted, preferred_element_type=jnp.float32
    )
    chunks = half.reshape(32, 2, 4, 16, 128).transpose(1, 2, 0, 3, 4).reshape(8, 512, 128)
    chunks = chunks.astype(jnp.bfloat16)
    parts = lax.all_to_all(chunks, "coef", 0, 0, tiled=True)
    reduced = jnp.sum(parts.astype(jnp.float32), axis=0).reshape(32, 16, 128)
    moved = lax.all_to_all(reduced, "pairs", 0, 0, tiled=True)
    owned = moved.reshape(32, 16, 2, 64)
    partly = jnp.einsum(
        "hqxy,yb->qhxb", owned, sig_panel.astype(jnp.float32), precision=lax.Precision.HIGHEST
    )
    lam = lam_panel.astype(jnp.float32).reshape(32, 2, 128)
    return jnp.einsum("hxa,qhxb->qab", lam, partly, precision=lax.Precision.HIGHEST)


def solution(mesh):
    placed = (
        P("pairs", "coef", None, None),
        P("pairs", "coef", None),
        P("pairs", "coef"),
        P(),
        P("coef", None),
        P("coef", None),
        P("coef", None),
    )
    return jax.shard_map(
        on_device,
        mesh=mesh,
        in_specs=placed,
        out_specs=P(("pairs", "coef"), None, None),
        check_vma=False,
    )
```

```python
import jax
import jax.numpy as jnp
from jax import lax
from jax.experimental import pallas as pl
from jax.experimental.pallas import tpu as pltpu
from jax.sharding import Mesh
from jax.sharding import PartitionSpec as P

f32 = jnp.float32
bf16 = jnp.bfloat16
COEF = ("zh", "zl")
BLOCK = 304
SPLIT = 160
PLACES = 0x54172630


def shift(x, k):
    return lax.ppermute(x, COEF, [(i, (i + k) % 8) for i in range(8)])


def relayout_kernel(x_ref, o_ref):
    o_ref[...] = jnp.swapaxes(x_ref[0], 0, 1)


def relayout(x):
    return pl.pallas_call(
        relayout_kernel,
        grid=(8,),
        in_specs=[pl.BlockSpec((1, 64, 64, 128), lambda s: (s, 0, 0, 0))],
        out_specs=pl.BlockSpec((64, 64, 128), lambda s: (0, s, 0)),
        out_shape=jax.ShapeDtypeStruct((64, 512, 128), bf16),
        compiler_params=pltpu.CompilerParams(vmem_limit_bytes=24 * 2**20),
        cost_estimate=pl.CostEstimate(flops=0, bytes_accessed=2**24, transcendentals=0),
    )(x)


STEP = 16
WIDE = 16


def transform_kernel(
    sc_ref, mine_ref, other_ref, x_ref, keep_ref, up1_ref, down1_ref, up2_ref, down2_ref, lhs_ref, cw_ref, q_ref
):
    n = pl.program_id(0)
    core = sc_ref[40]
    z = sc_ref[41]

    @pl.when(n == 0)
    def _():
        lane = lax.broadcasted_iota(jnp.int32, (64, 128), 1)

        def block(row, half, want):
            row = pl.multiple_of(row, 16)
            a = mine_ref[pl.ds(row, 32), :].astype(f32)
            b = other_ref[pl.ds(row, 32), :].astype(f32)
            t = jnp.concatenate([jnp.where(core == 0, a, b), jnp.where(core == 0, b, a)], axis=0)
            return jnp.where(half == want, t, pltpu.roll(t, 64, 1))

        def two(base, k):
            low = block(sc_ref[base + 2 * k], sc_ref[base + 8 + 2 * k], 0)
            high = block(sc_ref[base + 2 * k + 1], sc_ref[base + 9 + 2 * k], 1)
            return low, high

        rows, cols = [], []
        for k in range(4):
            low, high = two(0, k)
            rows.append(jnp.where(lane < 64, low, high).astype(bf16))
            low, high = two(16, k)
            low = low * sc_ref[32 + 2 * k].astype(f32)
            high = high * sc_ref[33 + 2 * k].astype(f32)
            cols.append(jnp.where(lane < 64, low, high).astype(bf16))
        rows = jnp.concatenate(rows, axis=1)
        cols = jnp.concatenate(cols, axis=1)
        r = lax.broadcasted_iota(jnp.int32, (512, 64), 0)
        c = lax.broadcasted_iota(jnp.int32, (512, 64), 1)
        spread = ((r >> 3) == c).astype(f32).astype(bf16)
        wide = jnp.dot(spread, rows, preferred_element_type=f32)
        r = lax.broadcasted_iota(jnp.int32, (512, 512), 0)
        c = lax.broadcasted_iota(jnp.int32, (512, 512), 1)
        lhs_ref[...] = jnp.where((r & 7) == (c >> 6), wide, 0.0).astype(bf16)
        order = (((r & 63) << 3) + (r >> 6) == c).astype(f32).astype(bf16)
        cw_ref[...] = jnp.dot(cols, order, preferred_element_type=f32).astype(bf16)

    def first(t, carry):
        rhs = jnp.concatenate([x_ref[WIDE * t + k] for k in range(WIDE)], axis=1)
        res = jnp.dot(lhs_ref[...], rhs, preferred_element_type=f32)
        for i in range(64):
            for k in range(WIDE // 2):
                a = res[i * 8 : i * 8 + 8, k * 256 : k * 256 + 128]
                b = res[i * 8 : i * 8 + 8, k * 256 + 128 : k * 256 + 256]
                row = pl.multiple_of(i * 512 + n * (STEP * 8) + t * (8 * WIDE) + k * 16, 16)
                q_ref[pl.ds(row, 16), :] = jnp.concatenate([a, b], axis=0).astype(bf16)
        return carry

    lax.fori_loop(0, STEP // WIDE, first, 0)

    @pl.when(n == 64 // STEP - 1)
    def _():
        cw = jnp.concatenate(
            [cw_ref[pl.ds(pl.multiple_of(lax.rem(z + e, 4) * 16, 16), 16), :] for e in range(4)], axis=0
        )

        def second(g, carry):
            rhs = jnp.concatenate(
                [q_ref[pl.ds(pl.multiple_of((g * 16 + k) * 512, 16), 512), :] for k in range(16)], axis=1
            )
            res = jnp.dot(cw, rhs, preferred_element_type=f32)
            for k in range(16):
                r = res[:, k * 128 : (k + 1) * 128]
                rows = pl.ds(pl.multiple_of(g * 256 + k * 16, 16), 16)
                keep_ref[rows, :] = r[0:16]
                up1_ref[rows, :] = r[16:32].astype(bf16)
                down1_ref[rows, :] = r[48:64].astype(bf16)

                @pl.when(g < 2)
                def _():
                    up2_ref[rows, :] = r[32:48].astype(bf16)

                @pl.when(g >= 2)
                def _():
                    rows = pl.ds(pl.multiple_of((g - 2) * 256 + k * 16, 16), 16)
                    down2_ref[rows, :] = r[32:48].astype(bf16)

            return carry

        lax.fori_loop(0, 4, second, 0)


def transform(scalars, mine, other, x):
    def whole(n, *_):
        return (0, 0)

    return pl.pallas_call(
        transform_kernel,
        grid_spec=pltpu.PrefetchScalarGridSpec(
            num_scalar_prefetch=1,
            grid=(64 // STEP,),
            in_specs=[
                pl.BlockSpec((8 * BLOCK, 128), whole),
                pl.BlockSpec((8 * BLOCK, 128), whole),
                pl.BlockSpec((STEP, 512, 128), lambda n, *_: (n, 0, 0)),
            ],
            out_specs=[pl.BlockSpec((1024, 128), whole)] * 3 + [pl.BlockSpec((512, 128), whole)] * 2,
            scratch_shapes=[
                pltpu.VMEM((512, 512), bf16),
                pltpu.VMEM((64, 512), bf16),
                pltpu.VMEM((64 * 512, 128), bf16),
            ],
        ),
        out_shape=[jax.ShapeDtypeStruct((1024, 128), f32)]
        + [jax.ShapeDtypeStruct((1024, 128), bf16)] * 2
        + [jax.ShapeDtypeStruct((512, 128), bf16)] * 2,
        compiler_params=pltpu.CompilerParams(vmem_limit_bytes=40 * 2**20),
        cost_estimate=pl.CostEstimate(flops=2**33, bytes_accessed=10 * 2**20, transcendentals=0),
    )(scalars, mine, other, x)


def split(x):
    high = x.astype(bf16)
    return high, (x - high.astype(f32)).astype(bf16)


def final_kernel(m_ref, lam_ref, sig_ref, o_ref, low_ref, high_ref):
    m = m_ref[...].astype(f32).reshape(32, 2, 16, 128)
    h = (m[:, 0] + m[:, 1]).reshape(512, 128)
    sig = sig_ref[...]
    zero = jnp.zeros_like(sig)
    pair = jnp.concatenate([jnp.concatenate([sig, zero], axis=1), jnp.concatenate([zero, sig], axis=1)], axis=0)
    pair = jnp.concatenate([pair, pair], axis=0)
    t = jnp.dot(jnp.concatenate(split(h), axis=1), pair, preferred_element_type=f32)
    low_ref[...] = t[:, :128]
    high_ref[...] = t[:, 128:]
    cols = []
    for q in range(16):
        low = low_ref[pl.ds(q, 32, stride=16), :]
        high = high_ref[pl.ds(q, 32, stride=16), :]
        cols.append(jnp.concatenate(split(jnp.concatenate([low, high], axis=0)), axis=0))
    lam = lam_ref[...]
    res = jnp.dot(jnp.concatenate([lam, lam], axis=1), jnp.concatenate(cols, axis=1), preferred_element_type=f32)
    for q in range(16):
        o_ref[q] = res[:, q * 128 : (q + 1) * 128]


def final(m, lam, sig):
    return pl.pallas_call(
        final_kernel,
        out_shape=jax.ShapeDtypeStruct((16, 128, 128), f32),
        scratch_shapes=[pltpu.VMEM((512, 128), f32)] * 2,
        compiler_params=pltpu.CompilerParams(vmem_limit_bytes=24 * 2**20),
        cost_estimate=pl.CostEstimate(flops=2**28, bytes_accessed=2**21, transcendentals=0),
    )(m, lam, sig)


def on_device(integrals, block_shells, live_counts, significance, occ_coef, lam_coef, sig_coef):
    core = lax.axis_index("pairs") % 2
    z = lax.axis_index(COEF)

    own = lax.dynamic_slice_in_dim(occ_coef.T, core * 32, 32, axis=0)
    own = own.reshape(32, 9, 128).transpose(1, 0, 2).reshape(288, 128)
    own = jnp.concatenate([own, lam_coef, sig_coef], axis=0)
    below = shift(own, 3)
    above = shift(own, -3)
    from_below = shift(jnp.concatenate([own, above, below[:SPLIT]], axis=0), 1)
    from_above = shift(jnp.concatenate([own, below, above[SPLIT:]], axis=0), -1)
    mine = jnp.concatenate(
        [own, below, above, from_above[: 2 * BLOCK], from_below, from_above[2 * BLOCK :]], axis=0
    )
    other = lax.ppermute(mine, "pairs", [(i, i ^ 1) for i in range(32)])

    x = relayout(integrals.transpose(1, 2, 3, 0))

    shells = block_shells[0].T
    owner = shells // 18
    inner = shells % 18
    place = (PLACES >> (4 * ((owner - z) % 8))) & 15
    rows = place * BLOCK + (inner // 2) * 32
    halves = inner % 2
    screened = significance[shells[0], shells[1]]
    live = ((jnp.arange(8) < live_counts[0, 0]) & (screened == 1)).astype(jnp.int32)
    scalars = jnp.concatenate(
        [rows[0], halves[0], rows[1], halves[1], live, jnp.stack([core, z]).astype(jnp.int32)]
    )

    keep, up1, down1, up2, down2 = transform(scalars, mine, other, x)
    near = shift(up1, 1).astype(f32) + shift(down1, -1).astype(f32)
    far = jnp.concatenate([shift(up2, 2), shift(down2, -2)], axis=0).astype(f32)
    summed = (keep + near + far).astype(bf16).reshape(64, 16, 128)
    moved = lax.all_to_all(summed, ("pairs", "zh"), 0, 0, tiled=True)

    panels = mine.reshape(8, BLOCK, 128)[:, 288:]
    place = (PLACES >> (4 * ((jnp.arange(8) - z) % 8))) & 15
    panels = panels[place]
    lam = panels[:, :8].reshape(32, 2, 128).transpose(2, 1, 0).reshape(128, 64)
    sig = panels[:, 8:].reshape(64, 128)
    return final(moved, lam, sig)


def solution(mesh):
    fine = Mesh(mesh.devices.reshape(32, 2, 4), ("pairs",) + COEF)
    placed = (
        P("pairs", COEF, None, None),
        P("pairs", COEF, None),
        P("pairs", COEF),
        P(),
        P(COEF, None),
        P(COEF, None),
        P(COEF, None),
    )
    return jax.shard_map(
        on_device,
        mesh=fine,
        in_specs=placed,
        out_specs=P(("pairs",) + COEF, None, None),
        check_vma=False,
    )
```

```python
import jax
import jax.numpy as jnp
from jax import lax
from jax.experimental import pallas as pl
from jax.experimental.pallas import tpu as pltpu
from jax.sharding import Mesh
from jax.sharding import PartitionSpec as P

f32 = jnp.float32
bf16 = jnp.bfloat16
COEF = ("zh", "zl")
BLOCK = 304
SPLIT = 160
PLACES = 0x54172630
ORDER = (0, 5, 3, 1, 6, 7, 2, 4)


def shift(x, k):
    return lax.ppermute(x, COEF, [(i, (i + k) % 8) for i in range(8)])


def relayout_kernel(x_ref, o_ref):
    s = pl.program_id(0)
    o_ref[:, pl.ds(pl.multiple_of(s * 64, 64), 64), :] = jnp.swapaxes(x_ref[0], 0, 1)


def relayout(x, part):
    return pl.pallas_call(
        relayout_kernel,
        grid=(4,),
        in_specs=[pl.BlockSpec((1, 64, 64, 128), lambda s: (4 * part + s, 0, 0, 0))],
        out_specs=pl.BlockSpec(memory_space=pltpu.VMEM),
        out_shape=jax.ShapeDtypeStruct((64, 256, 128), bf16),
        compiler_params=pltpu.CompilerParams(vmem_limit_bytes=16 * 2**20),
        cost_estimate=pl.CostEstimate(flops=0, bytes_accessed=2**23, transcendentals=0),
    )(pltpu.with_memory_space_constraint(x, pltpu.HBM))


WIDE = 16


def transform_kernel(
    shells_ref, count_ref, where_ref, screen_ref, mine_ref, other_ref, xa_ref, xb_ref,
    keep_ref, up1_ref, down1_ref, up2_ref, down2_ref, lam_ref, sig_ref,
    lhs_ref, cw_ref, q_ref,
):
    core = where_ref[0]
    z = where_ref[1]
    lane = lax.broadcasted_iota(jnp.int32, (64, 128), 1)

    def block(shell, want):
        inner = lax.rem(shell, 18)
        place = (PLACES >> (4 * ((lax.div(shell, 18) - z) & 7))) & 15
        row = pl.multiple_of(place * BLOCK + (inner >> 1) * 32, 16)
        a = mine_ref[pl.ds(row, 32), :].astype(f32)
        b = other_ref[pl.ds(row, 32), :].astype(f32)
        t = jnp.concatenate([jnp.where(core == 0, a, b), jnp.where(core == 0, b, a)], axis=0)
        return jnp.where((inner & 1) == want, t, pltpu.roll(t, 64, 1))

    def weighted(k, want):
        m = shells_ref[0, k, 0]
        n = shells_ref[0, k, 1]
        row = screen_ref[pl.ds(m, 1), :]
        at = lax.broadcasted_iota(jnp.int32, (1, 144), 1) == n
        live = jnp.sum(jnp.where(at, row, 0), axis=1, keepdims=True) == 1
        live = live & (k < count_ref[0, 0])
        return jnp.where(live, block(n, want), 0.0)

    rows, cols = [], []
    for k in range(4):
        low, high = block(shells_ref[0, 2 * k, 0], 0), block(shells_ref[0, 2 * k + 1, 0], 1)
        rows.append(jnp.where(lane < 64, low, high).astype(bf16))
        low, high = weighted(2 * k, 0), weighted(2 * k + 1, 1)
        cols.append(jnp.where(lane < 64, low, high).astype(bf16))
    rows = jnp.concatenate(rows, axis=1)
    cols = jnp.concatenate(cols, axis=1)
    r = lax.broadcasted_iota(jnp.int32, (512, 64), 0)
    c = lax.broadcasted_iota(jnp.int32, (512, 64), 1)
    spread = ((r >> 3) == c).astype(f32).astype(bf16)
    wide = jnp.dot(spread, rows, preferred_element_type=f32)
    r = lax.broadcasted_iota(jnp.int32, (512, 512), 0)
    c = lax.broadcasted_iota(jnp.int32, (512, 512), 1)
    lhs_ref[...] = jnp.where((r & 7) == (c >> 6), wide, 0.0).astype(bf16)
    r = lax.broadcasted_iota(jnp.int32, (512, 1024), 0)
    c = lax.broadcasted_iota(jnp.int32, (512, 1024), 1)
    order = (((r & 63) << 3) + (r >> 6) == ((c >> 4) << 3) + (c & 7)).astype(f32).astype(bf16)
    both = jnp.dot(cols, order, preferred_element_type=f32)
    odd = ((lax.broadcasted_iota(jnp.int32, (64, 1024), 1) >> 3) & 1) == 1
    cw_ref[0:64, :] = jnp.where(odd, 0.0, both).astype(bf16)
    cw_ref[64:128, :] = jnp.where(odd, both, 0.0).astype(bf16)
    for k, d in enumerate(ORDER):
        p = mine_ref[k * BLOCK + 288 : k * BLOCK + 304, :].astype(f32)
        to = pl.ds(pl.multiple_of(((z + d) & 7) * 8, 8), 8)
        lam_ref[to, :] = p[:8]
        sig_ref[to, :] = p[8:]

    def first(t, carry):
        rhs = jnp.concatenate(
            [
                jnp.concatenate([x_ref[WIDE * t + k] for k in range(WIDE)], axis=1)
                for x_ref in (xa_ref, xb_ref)
            ],
            axis=0,
        )
        res = jnp.dot(lhs_ref[...], rhs, preferred_element_type=f32).astype(bf16)
        for i in range(32):
            for k in range(WIDE):
                row = pl.multiple_of(i * 1024 + t * (16 * WIDE) + k * 16, 16)
                q_ref[pl.ds(row, 16), :] = res[i * 16 : (i + 1) * 16, k * 128 : (k + 1) * 128]
        return carry

    lax.fori_loop(0, 64 // WIDE, first, 0, unroll=True)

    cw = jnp.concatenate(
        [
            cw_ref[pl.ds(pl.multiple_of(h * 64 + ((z + e) & 3) * 16, 16), 16), :]
            for h in range(2)
            for e in range(4)
        ],
        axis=0,
    )
    for g in range(2):
        rhs = jnp.concatenate([q_ref[(g * 16 + k) * 1024 : (g * 16 + k + 1) * 1024, :] for k in range(16)], axis=1)
        res = jnp.dot(cw, rhs, preferred_element_type=f32)
        for k in range(16):
            for h in range(2):
                r = res[h * 64 : (h + 1) * 64, k * 128 : (k + 1) * 128]
                at = k * 32 + h * 16
                to = slice(g * 512 + at, g * 512 + at + 16)
                keep_ref[to, :] = r[0:16]
                up1_ref[to, :] = r[16:32].astype(bf16)
                down1_ref[to, :] = r[48:64].astype(bf16)
                (up2_ref, down2_ref)[g][at : at + 16, :] = r[32:48].astype(bf16)


def transform(shells, count, where, screen, mine, other, *x):
    scalar = pl.BlockSpec(memory_space=pltpu.SMEM)
    vector = pl.BlockSpec(memory_space=pltpu.VMEM)
    return pl.pallas_call(
        transform_kernel,
        in_specs=[scalar] * 3 + [vector] * 5,
        out_specs=[vector] * 7,
        scratch_shapes=[
            pltpu.VMEM((512, 512), bf16),
            pltpu.VMEM((128, 1024), bf16),
            pltpu.VMEM((32 * 1024, 128), bf16),
        ],
        out_shape=[jax.ShapeDtypeStruct((1024, 128), f32)]
        + [jax.ShapeDtypeStruct((1024, 128), bf16)] * 2
        + [jax.ShapeDtypeStruct((512, 128), bf16)] * 2
        + [jax.ShapeDtypeStruct((64, 128), f32)] * 2,
        compiler_params=pltpu.CompilerParams(vmem_limit_bytes=40 * 2**20),
        cost_estimate=pl.CostEstimate(flops=2**33, bytes_accessed=10 * 2**20, transcendentals=0),
    )(shells, count, where, screen, mine, other, *(pltpu.with_memory_space_constraint(t, pltpu.VMEM) for t in x))


def split(x):
    high = x.astype(bf16)
    return high, (x - high.astype(f32)).astype(bf16)


def final_kernel(m_ref, lam_ref, sig_ref, o_ref, low_ref, high_ref):
    m = m_ref[...].astype(f32).reshape(32, 2, 16, 128)
    h = (m[:, 0] + m[:, 1]).reshape(512, 128)
    sig = sig_ref[...].astype(bf16)
    zero = jnp.zeros_like(sig)
    pair = jnp.concatenate([jnp.concatenate([sig, zero], axis=1), jnp.concatenate([zero, sig], axis=1)], axis=0)
    pair = jnp.concatenate([pair, pair], axis=0)
    t = jnp.dot(jnp.concatenate(split(h), axis=1), pair, preferred_element_type=f32)
    low_ref[...] = t[:, :128]
    high_ref[...] = t[:, 128:]
    cols = []
    for q in range(16):
        low = low_ref[pl.ds(q, 32, stride=16), :]
        high = high_ref[pl.ds(q, 32, stride=16), :]
        cols.append(jnp.concatenate(split(jnp.concatenate([low, high], axis=0)), axis=0))
    lam = jnp.concatenate([lam_ref[pl.ds(k, 32, stride=2), :] for k in (0, 1)] * 2, axis=0).astype(bf16)
    res = lax.dot_general(lam, jnp.concatenate(cols, axis=1), (((0,), (0,)), ((), ())), preferred_element_type=f32)
    for q in range(16):
        o_ref[q] = res[:, q * 128 : (q + 1) * 128]


def final(m, lam, sig):
    return pl.pallas_call(
        final_kernel,
        out_shape=jax.ShapeDtypeStruct((16, 128, 128), f32),
        scratch_shapes=[pltpu.VMEM((512, 128), f32)] * 2,
        compiler_params=pltpu.CompilerParams(vmem_limit_bytes=24 * 2**20),
        cost_estimate=pl.CostEstimate(flops=2**28, bytes_accessed=2**21, transcendentals=0),
    )(m, lam, sig)


def on_device(integrals, block_shells, live_counts, significance, occ_coef, lam_coef, sig_coef):
    core = lax.axis_index("pairs") % 2
    z = lax.axis_index(COEF)

    own = lax.dynamic_slice_in_dim(occ_coef.T, core * 32, 32, axis=0)
    own = own.reshape(32, 9, 128).transpose(1, 0, 2).reshape(288, 128)
    own = jnp.concatenate([own, lam_coef, sig_coef], axis=0)
    below = shift(own, 3)
    above = shift(own, -3)
    x = integrals.transpose(1, 2, 3, 0)
    below, above, x_first = lax.optimization_barrier((below, above, relayout(x, 0)))
    from_below = shift(jnp.concatenate([own, above, below[:SPLIT]], axis=0), 1)
    from_above = shift(jnp.concatenate([own, below, above[SPLIT:]], axis=0), -1)
    from_below, from_above, x_second = lax.optimization_barrier((from_below, from_above, relayout(x, 1)))
    mine = jnp.concatenate(
        [own, below, above, from_above[: 2 * BLOCK], from_below, from_above[2 * BLOCK :]], axis=0
    )
    other = lax.ppermute(mine, "pairs", [(i, i ^ 1) for i in range(32)])

    where = jnp.stack([core, z]).astype(jnp.int32)
    keep, up1, down1, up2, down2, lam, sig = transform(
        block_shells, live_counts, where, significance, mine, other, x_first, x_second
    )
    near = shift(up1, 1).astype(f32) + shift(down1, -1).astype(f32)
    far = jnp.concatenate([shift(up2, 2), shift(down2, -2)], axis=0).astype(f32)
    summed = (keep + near + far).astype(bf16).reshape(64, 16, 128)
    moved = lax.all_to_all(summed, ("pairs", "zh"), 0, 0, tiled=True)

    return final(moved, lam, sig)


def solution(mesh):
    fine = Mesh(mesh.devices.reshape(32, 2, 4), ("pairs",) + COEF)
    placed = (
        P("pairs", COEF, None, None),
        P("pairs", COEF, None),
        P("pairs", COEF),
        P(),
        P(COEF, None),
        P(COEF, None),
        P(COEF, None),
    )
    return jax.shard_map(
        on_device,
        mesh=fine,
        in_specs=placed,
        out_specs=P(("pairs",) + COEF, None, None),
        check_vma=False,
    )
```

```python
import jax
import jax.numpy as jnp
from jax import lax
from jax.experimental import pallas as pl
from jax.experimental.pallas import tpu as pltpu
from jax.sharding import Mesh
from jax.sharding import PartitionSpec as P

f32 = jnp.float32
bf16 = jnp.bfloat16
COEF = ("zh", "zl")
BLOCK = 304
SPLIT = 160
PLACES = 0x54172630
ORDER = (0, 5, 3, 1, 6, 7, 2, 4)


def shift(x, k):
    return lax.ppermute(x, COEF, [(i, (i + k) % 8) for i in range(8)])


def relayout_kernel(where_ref, x_ref, o_ref):
    del where_ref
    s = pl.program_id(0)
    o_ref[:, pl.ds(pl.multiple_of(s * 64, 64), 64), :] = jnp.swapaxes(x_ref[0], 0, 1)


def relayout(where, x, part):
    return pl.pallas_call(
        relayout_kernel,
        grid=(4,),
        in_specs=[
            pl.BlockSpec(memory_space=pltpu.SMEM),
            pl.BlockSpec((1, 64, 64, 128), lambda s: (4 * part + s, 0, 0, 0)),
        ],
        out_specs=pl.BlockSpec(memory_space=pltpu.VMEM),
        out_shape=jax.ShapeDtypeStruct((64, 256, 128), bf16),
        compiler_params=pltpu.CompilerParams(vmem_limit_bytes=16 * 2**20),
        cost_estimate=pl.CostEstimate(flops=0, bytes_accessed=2**23, transcendentals=0),
    )(where, pltpu.with_memory_space_constraint(x, pltpu.HBM))


WIDE = 16


def transform_kernel(
    shells_ref, count_ref, where_ref, screen_ref, mine_ref, other_ref, xa_ref, xb_ref,
    keep_ref, up1_ref, down1_ref, up2_ref, down2_ref, lam_ref, sig_ref,
    lhs_ref, cw_ref, q_ref,
):
    core = where_ref[0]
    z = where_ref[1]
    lane = lax.broadcasted_iota(jnp.int32, (64, 128), 1)

    def block(shell, want):
        inner = lax.rem(shell, 18)
        place = (PLACES >> (4 * ((lax.div(shell, 18) - z) & 7))) & 15
        row = pl.multiple_of(place * BLOCK + (inner >> 1) * 32, 16)
        a = mine_ref[pl.ds(row, 32), :].astype(f32)
        b = other_ref[pl.ds(row, 32), :].astype(f32)
        t = jnp.concatenate([jnp.where(core == 0, a, b), jnp.where(core == 0, b, a)], axis=0)
        return jnp.where((inner & 1) == want, t, pltpu.roll(t, 64, 1))

    def weighted(k, want):
        m = shells_ref[0, 0, k]
        n = shells_ref[0, 1, k]
        row = screen_ref[pl.ds(m, 1), :]
        at = lax.broadcasted_iota(jnp.int32, (1, 144), 1) == n
        live = jnp.sum(jnp.where(at, row, 0), axis=1, keepdims=True) == 1
        live = live & (k < count_ref[0, 0])
        return jnp.where(live, block(n, want), 0.0)

    rows, cols = [], []
    for k in range(4):
        low, high = block(shells_ref[0, 0, 2 * k], 0), block(shells_ref[0, 0, 2 * k + 1], 1)
        rows.append(jnp.where(lane < 64, low, high).astype(bf16))
        low, high = weighted(2 * k, 0), weighted(2 * k + 1, 1)
        cols.append(jnp.where(lane < 64, low, high).astype(bf16))
    rows = jnp.concatenate(rows, axis=1)
    cols = jnp.concatenate(cols, axis=1)
    r = lax.broadcasted_iota(jnp.int32, (512, 64), 0)
    c = lax.broadcasted_iota(jnp.int32, (512, 64), 1)
    spread = ((r >> 3) == c).astype(f32).astype(bf16)
    wide = jnp.dot(spread, rows, preferred_element_type=f32)
    r = lax.broadcasted_iota(jnp.int32, (512, 512), 0)
    c = lax.broadcasted_iota(jnp.int32, (512, 512), 1)
    lhs_ref[...] = jnp.where((r & 7) == (c >> 6), wide, 0.0).astype(bf16)
    r = lax.broadcasted_iota(jnp.int32, (512, 1024), 0)
    c = lax.broadcasted_iota(jnp.int32, (512, 1024), 1)
    order = (((r & 63) << 3) + (r >> 6) == ((c >> 4) << 3) + (c & 7)).astype(f32).astype(bf16)
    both = jnp.dot(cols, order, preferred_element_type=f32)
    odd = ((lax.broadcasted_iota(jnp.int32, (64, 1024), 1) >> 3) & 1) == 1
    cw_ref[0:64, :] = jnp.where(odd, 0.0, both).astype(bf16)
    cw_ref[64:128, :] = jnp.where(odd, both, 0.0).astype(bf16)
    for k, d in enumerate(ORDER):
        p = mine_ref[k * BLOCK + 288 : k * BLOCK + 304, :].astype(f32)
        to = pl.ds(pl.multiple_of(((z + d) & 7) * 8, 8), 8)
        lam_ref[to, :] = p[:8]
        sig_ref[to, :] = p[8:]

    def first(t, carry):
        rhs = jnp.concatenate(
            [
                jnp.concatenate([x_ref[WIDE * t + k] for k in range(WIDE)], axis=1)
                for x_ref in (xa_ref, xb_ref)
            ],
            axis=0,
        )
        res = jnp.dot(lhs_ref[...], rhs, preferred_element_type=f32).astype(bf16)
        for i in range(32):
            for k in range(WIDE):
                row = pl.multiple_of(i * 1024 + t * (16 * WIDE) + k * 16, 16)
                q_ref[pl.ds(row, 16), :] = res[i * 16 : (i + 1) * 16, k * 128 : (k + 1) * 128]
        return carry

    lax.fori_loop(0, 64 // WIDE, first, 0, unroll=True)

    cw = jnp.concatenate(
        [
            cw_ref[pl.ds(pl.multiple_of(h * 64 + ((z + e) & 3) * 16, 16), 16), :]
            for h in range(2)
            for e in range(4)
        ],
        axis=0,
    )
    for g in range(2):
        rhs = jnp.concatenate([q_ref[(g * 16 + k) * 1024 : (g * 16 + k + 1) * 1024, :] for k in range(16)], axis=1)
        res = jnp.dot(cw, rhs, preferred_element_type=f32)
        for k in range(16):
            for h in range(2):
                r = res[h * 64 : (h + 1) * 64, k * 128 : (k + 1) * 128]
                at = k * 32 + h * 16
                to = slice(g * 512 + at, g * 512 + at + 16)
                keep_ref[to, :] = r[0:16]
                up1_ref[to, :] = r[16:32].astype(bf16)
                down1_ref[to, :] = r[48:64].astype(bf16)
                (up2_ref, down2_ref)[g][at : at + 16, :] = r[32:48].astype(bf16)


def transform(shells, count, where, screen, mine, other, *x):
    scalar = pl.BlockSpec(memory_space=pltpu.SMEM)
    vector = pl.BlockSpec(memory_space=pltpu.VMEM)
    return pl.pallas_call(
        transform_kernel,
        in_specs=[scalar] * 3 + [vector] * 5,
        out_specs=[vector] * 7,
        scratch_shapes=[
            pltpu.VMEM((512, 512), bf16),
            pltpu.VMEM((128, 1024), bf16),
            pltpu.VMEM((32 * 1024, 128), bf16),
        ],
        out_shape=[jax.ShapeDtypeStruct((1024, 128), f32)]
        + [jax.ShapeDtypeStruct((1024, 128), bf16)] * 2
        + [jax.ShapeDtypeStruct((512, 128), bf16)] * 2
        + [jax.ShapeDtypeStruct((64, 128), f32)] * 2,
        compiler_params=pltpu.CompilerParams(vmem_limit_bytes=40 * 2**20),
        cost_estimate=pl.CostEstimate(flops=2**33, bytes_accessed=10 * 2**20, transcendentals=0),
    )(shells, count, where, screen, mine, other, *(pltpu.with_memory_space_constraint(t, pltpu.VMEM) for t in x))


def split(x):
    high = x.astype(bf16)
    return high, (x - high.astype(f32)).astype(bf16)


def final_kernel(m_ref, lam_ref, sig_ref, o_ref, low_ref, high_ref):
    m = m_ref[...].astype(f32).reshape(32, 2, 16, 128)
    h = (m[:, 0] + m[:, 1]).reshape(512, 128)
    sig = sig_ref[...].astype(bf16)
    zero = jnp.zeros_like(sig)
    pair = jnp.concatenate([jnp.concatenate([sig, zero], axis=1), jnp.concatenate([zero, sig], axis=1)], axis=0)
    pair = jnp.concatenate([pair, pair], axis=0)
    t = jnp.dot(jnp.concatenate(split(h), axis=1), pair, preferred_element_type=f32)
    low_ref[...] = t[:, :128]
    high_ref[...] = t[:, 128:]
    cols = []
    for q in range(16):
        low = low_ref[pl.ds(q, 32, stride=16), :]
        high = high_ref[pl.ds(q, 32, stride=16), :]
        cols.append(jnp.concatenate(split(jnp.concatenate([low, high], axis=0)), axis=0))
    lam = jnp.concatenate([lam_ref[pl.ds(k, 32, stride=2), :] for k in (0, 1)] * 2, axis=0).astype(bf16)
    res = lax.dot_general(lam, jnp.concatenate(cols, axis=1), (((0,), (0,)), ((), ())), preferred_element_type=f32)
    for q in range(16):
        o_ref[q] = res[:, q * 128 : (q + 1) * 128]


def final(m, lam, sig):
    return pl.pallas_call(
        final_kernel,
        out_shape=jax.ShapeDtypeStruct((16, 128, 128), f32),
        scratch_shapes=[pltpu.VMEM((512, 128), f32)] * 2,
        compiler_params=pltpu.CompilerParams(vmem_limit_bytes=24 * 2**20),
        cost_estimate=pl.CostEstimate(flops=2**28, bytes_accessed=2**21, transcendentals=0),
    )(m, lam, sig)


def on_device(integrals, block_shells, live_counts, significance, occ_coef, lam_coef, sig_coef):
    core = lax.axis_index("pairs") % 2
    z = lax.axis_index(COEF)
    where = jnp.stack([core, z]).astype(jnp.int32)

    own = lax.dynamic_slice_in_dim(occ_coef.T, core * 32, 32, axis=0)
    own = own.reshape(32, 9, 128).transpose(1, 0, 2).reshape(288, 128)
    own = jnp.concatenate([own, lam_coef, sig_coef], axis=0)
    below = shift(own, 3)
    above = shift(own, -3)
    x = integrals.transpose(1, 2, 3, 0)
    below, above, x_first = lax.optimization_barrier((below, above, relayout(where, x, 0)))
    from_below = shift(jnp.concatenate([own, above, below[:SPLIT]], axis=0), 1)
    from_above = shift(jnp.concatenate([own, below, above[SPLIT:]], axis=0), -1)
    from_below, from_above, x_second = lax.optimization_barrier((from_below, from_above, relayout(where, x, 1)))
    mine = jnp.concatenate(
        [own, below, above, from_above[: 2 * BLOCK], from_below, from_above[2 * BLOCK :]], axis=0
    )
    other = lax.ppermute(mine, "pairs", [(i, i ^ 1) for i in range(32)])

    keep, up1, down1, up2, down2, lam, sig = transform(
        block_shells.transpose(0, 2, 1), live_counts, where, significance, mine, other, x_first, x_second
    )
    near = shift(up1, 1).astype(f32) + shift(down1, -1).astype(f32)
    far = jnp.concatenate([shift(up2, 2), shift(down2, -2)], axis=0).astype(f32)
    summed = (keep + near + far).astype(bf16).reshape(64, 16, 128)
    moved = lax.all_to_all(summed, ("pairs", "zh"), 0, 0, tiled=True)

    return final(moved, lam, sig)


def solution(mesh):
    fine = Mesh(mesh.devices.reshape(32, 2, 4), ("pairs",) + COEF)
    placed = (
        P("pairs", COEF, None, None),
        P("pairs", COEF, None),
        P("pairs", COEF),
        P(),
        P(COEF, None),
        P(COEF, None),
        P(COEF, None),
    )
    return jax.shard_map(
        on_device,
        mesh=fine,
        in_specs=placed,
        out_specs=P(("pairs",) + COEF, None, None),
        check_vma=False,
    )
```

```python
import jax
import jax.numpy as jnp
from jax import lax
from jax.experimental import pallas as pl
from jax.experimental.pallas import tpu as pltpu
from jax.sharding import Mesh
from jax.sharding import PartitionSpec as P

f32 = jnp.float32
bf16 = jnp.bfloat16
COEF = ("zh", "zl")
BLOCK = 304
SPLIT = 160
PLACES = 0x54172630
ORDER = (0, 5, 3, 1, 6, 7, 2, 4)


def shift(x, k):
    return lax.ppermute(x, COEF, [(i, (i + k) % 8) for i in range(8)])


def relayout_kernel(where_ref, x_ref, o_ref):
    del where_ref
    s = pl.program_id(0)
    o_ref[:, pl.ds(pl.multiple_of(s * 64, 64), 64), :] = jnp.swapaxes(x_ref[0], 0, 1)


def relayout(where, x, part):
    return pl.pallas_call(
        relayout_kernel,
        grid=(4,),
        in_specs=[
            pl.BlockSpec(memory_space=pltpu.SMEM),
            pl.BlockSpec((1, 64, 64, 128), lambda s: (4 * part + s, 0, 0, 0)),
        ],
        out_specs=pl.BlockSpec(memory_space=pltpu.VMEM),
        out_shape=jax.ShapeDtypeStruct((64, 256, 128), bf16),
        compiler_params=pltpu.CompilerParams(vmem_limit_bytes=16 * 2**20),
        cost_estimate=pl.CostEstimate(flops=0, bytes_accessed=2**23, transcendentals=0),
    )(where, pltpu.with_memory_space_constraint(x, pltpu.HBM))


WIDE = 16


def shell_block(shell, z, table_ref, want):
    inner = lax.rem(shell, 18)
    place = (PLACES >> (4 * ((lax.div(shell, 18) - z) & 7))) & 15
    row = pl.multiple_of(place * BLOCK + (inner >> 1) * 32, 16)
    t = table_ref[pl.ds(row, 32), :].astype(f32)
    return jnp.where((inner & 1) == want, t, pltpu.roll(t, 64, 1))


def first_product(shells_ref, z, table_ref, xa_ref, xb_ref, lhs_ref, q_ref):
    lane = lax.broadcasted_iota(jnp.int32, (32, 128), 1)
    rows = []
    for k in range(4):
        low = shell_block(shells_ref[0, 0, 2 * k], z, table_ref, 0)
        high = shell_block(shells_ref[0, 0, 2 * k + 1], z, table_ref, 1)
        rows.append(jnp.where(lane < 64, low, high).astype(bf16))
    rows = jnp.concatenate(rows, axis=1)
    r = lax.broadcasted_iota(jnp.int32, (256, 32), 0)
    c = lax.broadcasted_iota(jnp.int32, (256, 32), 1)
    spread = ((r >> 3) == c).astype(f32).astype(bf16)
    wide = jnp.dot(spread, rows, preferred_element_type=f32)
    r = lax.broadcasted_iota(jnp.int32, (256, 512), 0)
    c = lax.broadcasted_iota(jnp.int32, (256, 512), 1)
    lhs_ref[...] = jnp.where((r & 7) == (c >> 6), wide, 0.0).astype(bf16)

    def step(t, carry):
        rhs = jnp.concatenate(
            [
                jnp.concatenate([x_ref[WIDE * t + k] for k in range(WIDE)], axis=1)
                for x_ref in (xa_ref, xb_ref)
            ],
            axis=0,
        )
        res = jnp.dot(lhs_ref[...], rhs, preferred_element_type=f32).astype(bf16)
        for i in range(16):
            for k in range(WIDE):
                row = pl.multiple_of(i * 1024 + t * (16 * WIDE) + k * 16, 16)
                q_ref[pl.ds(row, 16), :] = res[i * 16 : (i + 1) * 16, k * 128 : (k + 1) * 128]
        return carry

    lax.fori_loop(0, 64 // WIDE, step, 0, unroll=True)


def second_product(z, cw_ref, q_ref, keep_ref, up, down):
    cw = jnp.concatenate(
        [cw_ref[pl.ds(pl.multiple_of(((z + d) & 7) * 16, 16), 16), :] for d in range(8)], axis=0
    )
    rhs = jnp.concatenate([q_ref[k * 1024 : (k + 1) * 1024, :] for k in range(16)], axis=1)
    res = jnp.dot(cw, rhs, preferred_element_type=f32)
    for k in range(16):
        for d in range(8):
            r = res[d * 16 : (d + 1) * 16, k * 128 : (k + 1) * 128]
            for ref, ds in ((keep_ref, (0, 3, 5)), up, down):
                if d in ds:
                    at = ds.index(d) * 256 + k * 16
                    ref[at : at + 16, :] = r.astype(ref.dtype)


SMEM = pl.BlockSpec(memory_space=pltpu.SMEM)
VMEM = pl.BlockSpec(memory_space=pltpu.VMEM)


def own_kernel(shells_ref, where_ref, mine_ref, xa_ref, xb_ref, q_ref, lam_ref, sig_ref, lhs_ref):
    z = where_ref[1]
    first_product(shells_ref, z, mine_ref, xa_ref, xb_ref, lhs_ref, q_ref)
    for k, d in enumerate(ORDER):
        p = mine_ref[k * BLOCK + 288 : k * BLOCK + 304, :].astype(f32)
        to = pl.ds(pl.multiple_of(((z + d) & 7) * 8, 8), 8)
        lam_ref[to, :] = p[:8]
        sig_ref[to, :] = p[8:]


def own_first(shells, where, mine, *x):
    return pl.pallas_call(
        own_kernel,
        in_specs=[SMEM] * 2 + [VMEM] * 3,
        out_specs=[VMEM] * 3,
        scratch_shapes=[pltpu.VMEM((256, 512), bf16)],
        out_shape=[jax.ShapeDtypeStruct((16 * 1024, 128), bf16)] + [jax.ShapeDtypeStruct((64, 128), f32)] * 2,
        compiler_params=pltpu.CompilerParams(vmem_limit_bytes=16 * 2**20),
        cost_estimate=pl.CostEstimate(flops=2**32, bytes_accessed=2**20, transcendentals=0),
    )(shells, where, mine, *(pltpu.with_memory_space_constraint(t, pltpu.VMEM) for t in x))


UP_OWN, DOWN_OWN = (1, 6, 4), (7, 2)
UP_OTHER, DOWN_OTHER = (1, 6), (7, 2, 4)


def columns_kernel(
    shells_ref, count_ref, where_ref, screen_ref, mine_ref, other_ref, q_ref, keep_ref, up_ref, down_ref, cw_ref
):
    core = where_ref[0]
    z = where_ref[1]
    lane = lax.broadcasted_iota(jnp.int32, (64, 128), 1)

    def weighted(k, want):
        m = shells_ref[0, 0, k]
        n = shells_ref[0, 1, k]
        row = screen_ref[pl.ds(m, 1), :]
        at = lax.broadcasted_iota(jnp.int32, (1, 144), 1) == n
        live = jnp.sum(jnp.where(at, row, 0), axis=1, keepdims=True) == 1
        live = live & (k < count_ref[0, 0])
        a = shell_block(n, z, mine_ref, want)
        b = shell_block(n, z, other_ref, want)
        t = jnp.concatenate([jnp.where(core == 0, a, b), jnp.where(core == 0, b, a)], axis=0)
        return jnp.where(live, t, 0.0)

    cols = []
    for k in range(4):
        low, high = weighted(2 * k, 0), weighted(2 * k + 1, 1)
        cols.append(jnp.where(lane < 64, low, high).astype(bf16))
    cols = jnp.concatenate(cols, axis=1)
    r = lax.broadcasted_iota(jnp.int32, (512, 1024), 0)
    c = lax.broadcasted_iota(jnp.int32, (512, 1024), 1)
    order = (((r & 63) << 3) + (r >> 6) == ((c >> 4) << 3) + (c & 7)).astype(f32).astype(bf16)
    both = jnp.dot(cols, order, preferred_element_type=f32)
    odd = ((lax.broadcasted_iota(jnp.int32, (64, 1024), 1) >> 3) & 1) == 1
    cw_ref[0:64, :] = jnp.where(odd, 0.0, both).astype(bf16)
    cw_ref[64:128, :] = jnp.where(odd, both, 0.0).astype(bf16)
    second_product(z, cw_ref, q_ref, keep_ref, (up_ref, UP_OWN), (down_ref, DOWN_OWN))


def own_second(shells, count, where, screen, mine, other, q):
    return pl.pallas_call(
        columns_kernel,
        in_specs=[SMEM] * 3 + [VMEM] * 4,
        out_specs=[VMEM] * 4,
        out_shape=[
            jax.ShapeDtypeStruct((768, 128), f32),
            jax.ShapeDtypeStruct((256 * len(UP_OWN), 128), bf16),
            jax.ShapeDtypeStruct((256 * len(DOWN_OWN), 128), bf16),
            jax.ShapeDtypeStruct((128, 1024), bf16),
        ],
        compiler_params=pltpu.CompilerParams(vmem_limit_bytes=16 * 2**20),
        cost_estimate=pl.CostEstimate(flops=2**31, bytes_accessed=2**20, transcendentals=0),
    )(shells, count, where, screen, mine, other, pltpu.with_memory_space_constraint(q, pltpu.VMEM))


def other_kernel(
    shells_ref, where_ref, other_ref, cw_ref, xa_ref, xb_ref, keep_ref, up_ref, down_ref, lhs_ref, q_ref
):
    z = where_ref[1]
    first_product(shells_ref, z, other_ref, xa_ref, xb_ref, lhs_ref, q_ref)
    second_product(z, cw_ref, q_ref, keep_ref, (up_ref, UP_OTHER), (down_ref, DOWN_OTHER))


def other_both(shells, where, other, cw, *x):
    return pl.pallas_call(
        other_kernel,
        in_specs=[SMEM] * 2 + [VMEM] * 4,
        out_specs=[VMEM] * 3,
        out_shape=[
            jax.ShapeDtypeStruct((768, 128), f32),
            jax.ShapeDtypeStruct((256 * len(UP_OTHER), 128), bf16),
            jax.ShapeDtypeStruct((256 * len(DOWN_OTHER), 128), bf16),
        ],
        scratch_shapes=[pltpu.VMEM((256, 512), bf16), pltpu.VMEM((16 * 1024, 128), bf16)],
        compiler_params=pltpu.CompilerParams(vmem_limit_bytes=24 * 2**20),
        cost_estimate=pl.CostEstimate(flops=2**33, bytes_accessed=2**20, transcendentals=0),
    )(shells, where, other, cw, *(pltpu.with_memory_space_constraint(t, pltpu.VMEM) for t in x))


def first_round(up, down):
    return shift(up, 1), shift(down, -1)


def second_round(keep, up_ds, from_below, down_ds, from_above):
    total = {0: keep[:256], 3: keep[256:512], 5: keep[512:]}
    for ds, got, step in ((up_ds, from_below, -1), (down_ds, from_above, 1)):
        for k, d in enumerate(ds):
            to = (d + step) % 8
            total[to] = total[to] + got[k * 256 : (k + 1) * 256].astype(f32)
    return total[0], shift(total[3].astype(bf16), 3), shift(total[5].astype(bf16), -3)


def reduced(total, from_below, from_above):
    return total + from_below.astype(f32) + from_above.astype(f32)


def split(x):
    high = x.astype(bf16)
    return high, (x - high.astype(f32)).astype(bf16)


def final_kernel(m_ref, lam_ref, sig_ref, o_ref, low_ref, high_ref):
    h = m_ref[...].reshape(512, 128)
    sig = sig_ref[...].astype(bf16)
    zero = jnp.zeros_like(sig)
    pair = jnp.concatenate([jnp.concatenate([sig, zero], axis=1), jnp.concatenate([zero, sig], axis=1)], axis=0)
    pair = jnp.concatenate([pair, pair], axis=0)
    t = jnp.dot(jnp.concatenate(split(h), axis=1), pair, preferred_element_type=f32)
    low_ref[...] = t[:, :128]
    high_ref[...] = t[:, 128:]
    cols = []
    for q in range(16):
        low = low_ref[pl.ds(q, 32, stride=16), :]
        high = high_ref[pl.ds(q, 32, stride=16), :]
        cols.append(jnp.concatenate(split(jnp.concatenate([low, high], axis=0)), axis=0))
    lam = jnp.concatenate([lam_ref[pl.ds(k, 32, stride=2), :] for k in (0, 1)] * 2, axis=0).astype(bf16)
    res = lax.dot_general(lam, jnp.concatenate(cols, axis=1), (((0,), (0,)), ((), ())), preferred_element_type=f32)
    for q in range(16):
        o_ref[q] = res[:, q * 128 : (q + 1) * 128]


def final(m, lam, sig):
    return pl.pallas_call(
        final_kernel,
        out_shape=jax.ShapeDtypeStruct((16, 128, 128), f32),
        scratch_shapes=[pltpu.VMEM((512, 128), f32)] * 2,
        compiler_params=pltpu.CompilerParams(vmem_limit_bytes=24 * 2**20),
        cost_estimate=pl.CostEstimate(flops=2**28, bytes_accessed=2**21, transcendentals=0),
    )(m, lam, sig)


def on_device(integrals, block_shells, live_counts, significance, occ_coef, lam_coef, sig_coef):
    core = lax.axis_index("pairs") % 2
    z = lax.axis_index(COEF)
    where = jnp.stack([core, z]).astype(jnp.int32)

    own = lax.dynamic_slice_in_dim(occ_coef.T, core * 32, 32, axis=0)
    own = own.reshape(32, 9, 128).transpose(1, 0, 2).reshape(288, 128)
    own = jnp.concatenate([own, lam_coef, sig_coef], axis=0)
    below = shift(own, 3)
    above = shift(own, -3)
    x = integrals.transpose(1, 2, 3, 0)
    below, above, x_first = lax.optimization_barrier((below, above, relayout(where, x, 0)))
    from_below = shift(jnp.concatenate([own, above, below[:SPLIT]], axis=0), 1)
    from_above = shift(jnp.concatenate([own, below, above[SPLIT:]], axis=0), -1)
    from_below, from_above, x_second = lax.optimization_barrier((from_below, from_above, relayout(where, x, 1)))
    mine = jnp.concatenate(
        [own, below, above, from_above[: 2 * BLOCK], from_below, from_above[2 * BLOCK :]], axis=0
    )
    other = lax.ppermute(mine, "pairs", [(i, i ^ 1) for i in range(32)])

    shells = block_shells.transpose(0, 2, 1)
    q, lam, sig = own_first(shells, where, mine, x_first, x_second)
    keep, up, down, cw = own_second(shells, live_counts, where, significance, mine, other, q)
    own_got = first_round(up, down)
    keep_other, up, down = other_both(shells, where, other, cw, x_first, x_second)
    other_got = first_round(up, down)
    own_half = second_round(keep, UP_OWN, own_got[0], DOWN_OWN, own_got[1])
    other_half = second_round(keep_other, UP_OTHER, other_got[0], DOWN_OTHER, other_got[1])
    a = reduced(*own_half)
    b = reduced(*other_half)
    summed = jnp.concatenate([jnp.where(core == 0, a, b), jnp.where(core == 0, b, a)], axis=0)
    moved = lax.all_to_all(summed.reshape(32, 16, 128), "pairs", 0, 0, tiled=True)

    return final(moved, lam, sig)


def solution(mesh):
    fine = Mesh(mesh.devices.reshape(32, 2, 4), ("pairs",) + COEF)
    placed = (
        P("pairs", COEF, None, None),
        P("pairs", COEF, None),
        P("pairs", COEF),
        P(),
        P(COEF, None),
        P(COEF, None),
        P(COEF, None),
    )
    return jax.shard_map(
        on_device,
        mesh=fine,
        in_specs=placed,
        out_specs=P(("pairs",) + COEF, None, None),
        check_vma=False,
    )
```

```python
import jax
import jax.numpy as jnp
from jax import lax
from jax.experimental import pallas as pl
from jax.experimental.pallas import tpu as pltpu
from jax.sharding import Mesh
from jax.sharding import PartitionSpec as P

f32 = jnp.float32
bf16 = jnp.bfloat16
COEF = ("zh", "zl")
BLOCK = 304
SPLIT = 160
PLACES = 0x54172630
ORDER = (0, 5, 3, 1, 6, 7, 2, 4)


def swap(x, k):
    pairs = []
    for p in range(32):
        for z in range(8):
            way = 1 - 2 * ((z + p) % 2)
            pairs.append((p * 8 + z, p * 8 + (z + way * k) % 8))
    return lax.ppermute(x, ("pairs",) + COEF, pairs)


def relayout_kernel(where_ref, x_ref, o_ref):
    del where_ref
    s = pl.program_id(0)
    o_ref[:, pl.ds(pl.multiple_of(s * 64, 64), 64), :] = jnp.swapaxes(x_ref[0], 0, 1)


def relayout(where, x, part):
    return pl.pallas_call(
        relayout_kernel,
        grid=(4,),
        in_specs=[
            pl.BlockSpec(memory_space=pltpu.SMEM),
            pl.BlockSpec((1, 64, 64, 128), lambda s: (4 * part + s, 0, 0, 0)),
        ],
        out_specs=pl.BlockSpec(memory_space=pltpu.VMEM),
        out_shape=jax.ShapeDtypeStruct((64, 256, 128), bf16),
        compiler_params=pltpu.CompilerParams(vmem_limit_bytes=16 * 2**20),
        cost_estimate=pl.CostEstimate(flops=0, bytes_accessed=2**23, transcendentals=0),
    )(where, pltpu.with_memory_space_constraint(x, pltpu.HBM))


WIDE = 16


def shell_block(shell, z, way, table_ref, want):
    inner = lax.rem(shell, 18)
    place = (PLACES >> (4 * ((way * (lax.div(shell, 18) - z)) & 7))) & 15
    row = pl.multiple_of(place * BLOCK + (inner >> 1) * 32, 16)
    t = table_ref[pl.ds(row, 32), :].astype(f32)
    return jnp.where((inner & 1) == want, t, pltpu.roll(t, 64, 1))


def first_product(shells_ref, z, way, table_ref, xa_ref, xb_ref, lhs_ref, q_ref):
    lane = lax.broadcasted_iota(jnp.int32, (32, 128), 1)
    rows = []
    for k in range(4):
        low = shell_block(shells_ref[0, 0, 2 * k], z, way, table_ref, 0)
        high = shell_block(shells_ref[0, 0, 2 * k + 1], z, way, table_ref, 1)
        rows.append(jnp.where(lane < 64, low, high).astype(bf16))
    r = lax.broadcasted_iota(jnp.int32, (128, 32), 0)
    c = lax.broadcasted_iota(jnp.int32, (128, 32), 1)
    spread = ((r >> 2) == c).astype(f32).astype(bf16)
    r = lax.broadcasted_iota(jnp.int32, (128, 256), 0)
    c = lax.broadcasted_iota(jnp.int32, (128, 256), 1)
    for half in range(2):
        four = jnp.concatenate(rows[2 * half : 2 * half + 2], axis=1)
        wide = jnp.dot(spread, four, preferred_element_type=f32)
        lhs_ref[half * 128 : (half + 1) * 128, :] = jnp.where((r & 3) == (c >> 6), wide, 0.0).astype(bf16)

    def step(t, carry):
        for half, x_ref in enumerate((xa_ref, xb_ref)):
            rhs = jnp.concatenate([x_ref[WIDE * t + k] for k in range(WIDE)], axis=1)
            lhs = lhs_ref[half * 128 : (half + 1) * 128, :]
            res = jnp.dot(lhs, rhs, preferred_element_type=f32).astype(bf16)
            for g in range(8):
                for k in range(WIDE):
                    row = pl.multiple_of(g * 2048 + half * 1024 + t * (16 * WIDE) + k * 16, 16)
                    q_ref[pl.ds(row, 16), :] = res[g * 16 : (g + 1) * 16, k * 128 : (k + 1) * 128]
        return carry

    lax.fori_loop(0, 64 // WIDE, step, 0, unroll=True)


def second_product(z, way, cw_ref, q_ref, keep_ref, up, down):
    cw = jnp.concatenate(
        [
            cw_ref[pl.ds(pl.multiple_of(b * 128 + ((z + way * d) & 7) * 16, 16), 16), :]
            for b in range(2)
            for d in range(8)
        ],
        axis=0,
    )
    rhs = jnp.concatenate([q_ref[g * 2048 : (g + 1) * 2048, :] for g in range(8)], axis=1)
    res = jnp.dot(cw, rhs, preferred_element_type=f32)
    for g in range(8):
        for b in range(2):
            for d in range(8):
                r = res[b * 128 + d * 16 : b * 128 + (d + 1) * 16, g * 128 : (g + 1) * 128]
                for ref, ds in ((keep_ref, (0, 3, 5)), up, down):
                    if d in ds:
                        at = ds.index(d) * 256 + (g * 2 + b) * 16
                        ref[at : at + 16, :] = r.astype(ref.dtype)


SMEM = pl.BlockSpec(memory_space=pltpu.SMEM)
VMEM = pl.BlockSpec(memory_space=pltpu.VMEM)


def own_kernel(shells_ref, where_ref, mine_ref, xa_ref, xb_ref, q_ref, lam_ref, sig_ref, lhs_ref):
    z = where_ref[1]
    way = where_ref[2]
    first_product(shells_ref, z, way, mine_ref, xa_ref, xb_ref, lhs_ref, q_ref)
    for k, d in enumerate(ORDER):
        p = mine_ref[k * BLOCK + 288 : k * BLOCK + 304, :].astype(f32)
        to = pl.ds(pl.multiple_of(((z + way * d) & 7) * 8, 8), 8)
        lam_ref[to, :] = p[:8]
        sig_ref[to, :] = p[8:]


def own_first(shells, where, mine, *x):
    return pl.pallas_call(
        own_kernel,
        in_specs=[SMEM] * 2 + [VMEM] * 3,
        out_specs=[VMEM] * 3,
        scratch_shapes=[pltpu.VMEM((256, 256), bf16)],
        out_shape=[jax.ShapeDtypeStruct((16 * 1024, 128), bf16)] + [jax.ShapeDtypeStruct((64, 128), f32)] * 2,
        compiler_params=pltpu.CompilerParams(vmem_limit_bytes=16 * 2**20),
        cost_estimate=pl.CostEstimate(flops=2**32, bytes_accessed=2**20, transcendentals=0),
    )(shells, where, mine, *(pltpu.with_memory_space_constraint(t, pltpu.VMEM) for t in x))


UP_OWN, DOWN_OWN = (1, 6, 4), (7, 2)
UP_OTHER, DOWN_OTHER = UP_OWN, DOWN_OWN


def columns_kernel(
    shells_ref, count_ref, where_ref, screen_ref, mine_ref, other_ref, q_ref, keep_ref, up_ref, down_ref, cw_ref
):
    core = where_ref[0]
    z = where_ref[1]
    way = where_ref[2]
    lane = lax.broadcasted_iota(jnp.int32, (64, 128), 1)

    def weighted(k, want):
        m = shells_ref[0, 0, k]
        n = shells_ref[0, 1, k]
        row = screen_ref[pl.ds(m, 1), :]
        at = lax.broadcasted_iota(jnp.int32, (1, 144), 1) == n
        live = jnp.sum(jnp.where(at, row, 0), axis=1, keepdims=True) == 1
        live = live & (k < count_ref[0, 0])
        a = shell_block(n, z, way, mine_ref, want)
        b = shell_block(n, z, -way, other_ref, want)
        t = jnp.concatenate([jnp.where(core == 0, a, b), jnp.where(core == 0, b, a)], axis=0)
        return jnp.where(live, t, 0.0)

    cols = []
    for k in range(4):
        low, high = weighted(2 * k, 0), weighted(2 * k + 1, 1)
        cols.append(jnp.where(lane < 64, low, high).astype(bf16))
    r = lax.broadcasted_iota(jnp.int32, (256, 1024), 0)
    c = lax.broadcasted_iota(jnp.int32, (256, 1024), 1)
    order = (((r & 63) << 2) + (r >> 6) == ((c >> 4) << 2) + (c & 3)).astype(f32).astype(bf16)
    column = (lax.broadcasted_iota(jnp.int32, (64, 1024), 1) >> 2) & 3
    for half in range(2):
        four = jnp.concatenate(cols[2 * half : 2 * half + 2], axis=1)
        wide = jnp.dot(four, order, preferred_element_type=f32)
        for i in range(4):
            cw_ref[i * 64 : (i + 1) * 64, half * 1024 : (half + 1) * 1024] = jnp.where(
                column == i, wide, 0.0
            ).astype(bf16)
    second_product(z, way, cw_ref, q_ref, keep_ref, (up_ref, UP_OWN), (down_ref, DOWN_OWN))


def own_second(shells, count, where, screen, mine, other, q):
    return pl.pallas_call(
        columns_kernel,
        in_specs=[SMEM] * 3 + [VMEM] * 4,
        out_specs=[VMEM] * 4,
        out_shape=[
            jax.ShapeDtypeStruct((768, 128), f32),
            jax.ShapeDtypeStruct((256 * len(UP_OWN), 128), bf16),
            jax.ShapeDtypeStruct((256 * len(DOWN_OWN), 128), bf16),
            jax.ShapeDtypeStruct((256, 2048), bf16),
        ],
        compiler_params=pltpu.CompilerParams(vmem_limit_bytes=16 * 2**20),
        cost_estimate=pl.CostEstimate(flops=2**31, bytes_accessed=2**20, transcendentals=0),
    )(shells, count, where, screen, mine, other, pltpu.with_memory_space_constraint(q, pltpu.VMEM))


def other_kernel(
    shells_ref, where_ref, other_ref, cw_ref, xa_ref, xb_ref, keep_ref, up_ref, down_ref, lhs_ref, q_ref
):
    z = where_ref[1]
    way = where_ref[2]
    first_product(shells_ref, z, -way, other_ref, xa_ref, xb_ref, lhs_ref, q_ref)
    second_product(z, way, cw_ref, q_ref, keep_ref, (up_ref, UP_OTHER), (down_ref, DOWN_OTHER))


def other_both(shells, where, other, cw, *x):
    return pl.pallas_call(
        other_kernel,
        in_specs=[SMEM] * 2 + [VMEM] * 4,
        out_specs=[VMEM] * 3,
        out_shape=[
            jax.ShapeDtypeStruct((768, 128), f32),
            jax.ShapeDtypeStruct((256 * len(UP_OTHER), 128), bf16),
            jax.ShapeDtypeStruct((256 * len(DOWN_OTHER), 128), bf16),
        ],
        scratch_shapes=[pltpu.VMEM((256, 256), bf16), pltpu.VMEM((16 * 1024, 128), bf16)],
        compiler_params=pltpu.CompilerParams(vmem_limit_bytes=24 * 2**20),
        cost_estimate=pl.CostEstimate(flops=2**33, bytes_accessed=2**20, transcendentals=0),
    )(shells, where, other, cw, *(pltpu.with_memory_space_constraint(t, pltpu.VMEM) for t in x))


def first_round(up, down):
    return swap(up, 1), swap(down, -1)


def second_round(keep, up_ds, from_ahead, down_ds, from_behind):
    total = {0: keep[:256], 3: keep[256:512], 5: keep[512:]}
    for ds, got, step in ((up_ds, from_ahead, 1), (down_ds, from_behind, -1)):
        for k, d in enumerate(ds):
            to = (step - d) % 8
            total[to] = total[to] + got[k * 256 : (k + 1) * 256].astype(f32)
    return total[0], swap(total[3].astype(bf16), 3), swap(total[5].astype(bf16), -3)


def reduced(total, from_ahead, from_behind):
    return total + from_ahead.astype(f32) + from_behind.astype(f32)


def split(x):
    high = x.astype(bf16)
    return high, (x - high.astype(f32)).astype(bf16)


def final_kernel(m_ref, lam_ref, sig_ref, o_ref, low_ref, high_ref):
    h = m_ref[...].reshape(512, 128)
    sig = sig_ref[...].astype(bf16)
    zero = jnp.zeros_like(sig)
    pair = jnp.concatenate([jnp.concatenate([sig, zero], axis=1), jnp.concatenate([zero, sig], axis=1)], axis=0)
    pair = jnp.concatenate([pair, pair], axis=0)
    t = jnp.dot(jnp.concatenate(split(h), axis=1), pair, preferred_element_type=f32)
    low_ref[...] = t[:, :128]
    high_ref[...] = t[:, 128:]
    cols = []
    for q in range(16):
        low = low_ref[pl.ds(q, 32, stride=16), :]
        high = high_ref[pl.ds(q, 32, stride=16), :]
        cols.append(jnp.concatenate(split(jnp.concatenate([low, high], axis=0)), axis=0))
    lam = jnp.concatenate([lam_ref[pl.ds(k, 32, stride=2), :] for k in (0, 1)] * 2, axis=0).astype(bf16)
    res = lax.dot_general(lam, jnp.concatenate(cols, axis=1), (((0,), (0,)), ((), ())), preferred_element_type=f32)
    for q in range(16):
        o_ref[q] = res[:, q * 128 : (q + 1) * 128]


def final(m, lam, sig):
    return pl.pallas_call(
        final_kernel,
        out_shape=jax.ShapeDtypeStruct((16, 128, 128), f32),
        scratch_shapes=[pltpu.VMEM((512, 128), f32)] * 2,
        compiler_params=pltpu.CompilerParams(vmem_limit_bytes=24 * 2**20),
        cost_estimate=pl.CostEstimate(flops=2**28, bytes_accessed=2**21, transcendentals=0),
    )(m, lam, sig)


def on_device(integrals, block_shells, live_counts, significance, occ_coef, lam_coef, sig_coef):
    core = lax.axis_index("pairs") % 2
    z = lax.axis_index(COEF)
    where = jnp.stack([core, z, 1 - 2 * ((z + core) % 2)]).astype(jnp.int32)

    own = lax.dynamic_slice_in_dim(occ_coef.T, core * 32, 32, axis=0)
    own = own.reshape(32, 9, 128).transpose(1, 0, 2).reshape(288, 128)
    own = jnp.concatenate([own, lam_coef, sig_coef], axis=0)
    ahead = swap(own, 3)
    behind = swap(own, -3)
    x = integrals.transpose(1, 2, 3, 0)
    ahead, behind, x_first = lax.optimization_barrier((ahead, behind, relayout(where, x, 0)))
    from_ahead = swap(jnp.concatenate([own, ahead, behind[:SPLIT]], axis=0), 1)
    from_behind = swap(jnp.concatenate([own, behind, ahead[SPLIT:]], axis=0), -1)
    from_ahead, from_behind, x_second = lax.optimization_barrier((from_ahead, from_behind, relayout(where, x, 1)))
    near = 2 * BLOCK
    mine = jnp.concatenate(
        [own, behind, ahead, from_ahead[:near], from_behind[:near], from_ahead[near:], from_behind[near:]], axis=0
    )
    other = lax.ppermute(mine, "pairs", [(i, i ^ 1) for i in range(32)])

    shells = block_shells.transpose(0, 2, 1)
    q, lam, sig = own_first(shells, where, mine, x_first, x_second)
    keep, up, down, cw = own_second(shells, live_counts, where, significance, mine, other, q)
    own_got = first_round(up, down)
    keep_other, up, down = other_both(shells, where, other, cw, x_first, x_second)
    other_got = first_round(up, down)
    own_half = second_round(keep, UP_OWN, own_got[0], DOWN_OWN, own_got[1])
    other_half = second_round(keep_other, UP_OTHER, other_got[0], DOWN_OTHER, other_got[1])
    a = reduced(*own_half)
    b = reduced(*other_half)
    summed = jnp.concatenate([jnp.where(core == 0, a, b), jnp.where(core == 0, b, a)], axis=0)
    moved = lax.all_to_all(summed.reshape(32, 16, 128), "pairs", 0, 0, tiled=True)

    return final(moved, lam, sig)


def solution(mesh):
    fine = Mesh(mesh.devices.reshape(32, 2, 4), ("pairs",) + COEF)
    placed = (
        P("pairs", COEF, None, None),
        P("pairs", COEF, None),
        P("pairs", COEF),
        P(),
        P(COEF, None),
        P(COEF, None),
        P(COEF, None),
    )
    return jax.shard_map(
        on_device,
        mesh=fine,
        in_specs=placed,
        out_specs=P(("pairs",) + COEF, None, None),
        check_vma=False,
    )
```

```python
import jax
import jax.numpy as jnp
from jax import lax
from jax.experimental import pallas as pl
from jax.experimental.pallas import tpu as pltpu
from jax.sharding import Mesh
from jax.sharding import PartitionSpec as P

f32 = jnp.float32
bf16 = jnp.bfloat16
COEF = ("zh", "zl")
BLOCK = 304
SPLIT = 304
PLACES = 0x54172630
ORDER = (0, 5, 3, 1, 6, 7, 2, 4)


def swap(x, k):
    pairs = []
    for p in range(32):
        for z in range(8):
            way = 1 - 2 * ((z + p) % 2)
            pairs.append((p * 8 + z, p * 8 + (z + way * k) % 8))
    return lax.ppermute(x, ("pairs",) + COEF, pairs)


def relayout_kernel(where_ref, x_ref, o_ref):
    del where_ref
    s = pl.program_id(0)
    o_ref[:, pl.ds(pl.multiple_of(s * 64, 64), 64), :] = jnp.swapaxes(x_ref[0], 0, 1)


def relayout(where, x, part):
    return pl.pallas_call(
        relayout_kernel,
        grid=(4,),
        in_specs=[
            pl.BlockSpec(memory_space=pltpu.SMEM),
            pl.BlockSpec((1, 64, 64, 128), lambda s: (4 * part + s, 0, 0, 0)),
        ],
        out_specs=pl.BlockSpec(memory_space=pltpu.VMEM),
        out_shape=jax.ShapeDtypeStruct((64, 256, 128), bf16),
        compiler_params=pltpu.CompilerParams(vmem_limit_bytes=16 * 2**20),
        cost_estimate=pl.CostEstimate(flops=0, bytes_accessed=2**23, transcendentals=0),
    )(where, pltpu.with_memory_space_constraint(x, pltpu.HBM))


WIDE = 16


def shell_block(shell, z, way, table_ref, want):
    inner = lax.rem(shell, 18)
    place = (PLACES >> (4 * ((way * (lax.div(shell, 18) - z)) & 7))) & 15
    row = pl.multiple_of(place * BLOCK + (inner >> 1) * 32, 16)
    t = table_ref[pl.ds(row, 32), :].astype(f32)
    return jnp.where((inner & 1) == want, t, pltpu.roll(t, 64, 1))


def first_product(shells_ref, z, way, table_ref, xa_ref, xb_ref, lhs_ref, q_ref):
    lane = lax.broadcasted_iota(jnp.int32, (32, 128), 1)
    rows = []
    for k in range(4):
        low = shell_block(shells_ref[0, 0, 2 * k], z, way, table_ref, 0)
        high = shell_block(shells_ref[0, 0, 2 * k + 1], z, way, table_ref, 1)
        rows.append(jnp.where(lane < 64, low, high).astype(bf16))
    r = lax.broadcasted_iota(jnp.int32, (128, 32), 0)
    c = lax.broadcasted_iota(jnp.int32, (128, 32), 1)
    spread = ((r >> 2) == c).astype(f32).astype(bf16)
    r = lax.broadcasted_iota(jnp.int32, (128, 256), 0)
    c = lax.broadcasted_iota(jnp.int32, (128, 256), 1)
    for half in range(2):
        four = jnp.concatenate(rows[2 * half : 2 * half + 2], axis=1)
        wide = jnp.dot(spread, four, preferred_element_type=f32)
        lhs_ref[half * 128 : (half + 1) * 128, :] = jnp.where((r & 3) == (c >> 6), wide, 0.0).astype(bf16)

    def step(t, carry):
        for half, x_ref in enumerate((xa_ref, xb_ref)):
            rhs = jnp.concatenate([x_ref[WIDE * t + k] for k in range(WIDE)], axis=1)
            lhs = lhs_ref[half * 128 : (half + 1) * 128, :]
            res = jnp.dot(lhs, rhs, preferred_element_type=f32).astype(bf16)
            for g in range(8):
                for k in range(WIDE):
                    row = pl.multiple_of(g * 2048 + half * 1024 + t * (16 * WIDE) + k * 16, 16)
                    q_ref[pl.ds(row, 16), :] = res[g * 16 : (g + 1) * 16, k * 128 : (k + 1) * 128]
        return carry

    lax.fori_loop(0, 64 // WIDE, step, 0, unroll=True)


def second_product(z, way, cw_ref, q_ref, keep_ref, up, down):
    cw = jnp.concatenate(
        [
            cw_ref[pl.ds(pl.multiple_of(b * 128 + ((z + way * d) & 7) * 16, 16), 16), :]
            for b in range(2)
            for d in range(8)
        ],
        axis=0,
    )
    rhs = jnp.concatenate([q_ref[g * 2048 : (g + 1) * 2048, :] for g in range(8)], axis=1)
    res = jnp.dot(cw, rhs, preferred_element_type=f32)
    for g in range(8):
        for b in range(2):
            for d in range(8):
                r = res[b * 128 + d * 16 : b * 128 + (d + 1) * 16, g * 128 : (g + 1) * 128]
                for ref, ds in ((keep_ref, (0, 3, 5)), up, down):
                    if d in ds:
                        at = ds.index(d) * 256 + (g * 2 + b) * 16
                        ref[at : at + 16, :] = r.astype(ref.dtype)


SMEM = pl.BlockSpec(memory_space=pltpu.SMEM)
VMEM = pl.BlockSpec(memory_space=pltpu.VMEM)


def own_kernel(shells_ref, where_ref, mine_ref, xa_ref, xb_ref, q_ref, lam_ref, sig_ref, lhs_ref):
    z = where_ref[1]
    way = where_ref[2]
    first_product(shells_ref, z, way, mine_ref, xa_ref, xb_ref, lhs_ref, q_ref)
    for k, d in enumerate(ORDER):
        p = mine_ref[k * BLOCK + 288 : k * BLOCK + 304, :].astype(f32)
        to = pl.ds(pl.multiple_of(((z + way * d) & 7) * 8, 8), 8)
        lam_ref[to, :] = p[:8]
        sig_ref[to, :] = p[8:]


def own_first(shells, where, mine, *x):
    return pl.pallas_call(
        own_kernel,
        in_specs=[SMEM] * 2 + [VMEM] * 3,
        out_specs=[VMEM] * 3,
        scratch_shapes=[pltpu.VMEM((256, 256), bf16)],
        out_shape=[jax.ShapeDtypeStruct((16 * 1024, 128), bf16)] + [jax.ShapeDtypeStruct((64, 128), f32)] * 2,
        compiler_params=pltpu.CompilerParams(vmem_limit_bytes=16 * 2**20),
        cost_estimate=pl.CostEstimate(flops=2**32, bytes_accessed=2**20, transcendentals=0),
    )(shells, where, mine, *(pltpu.with_memory_space_constraint(t, pltpu.VMEM) for t in x))


UP_OWN, DOWN_OWN = (1, 6, 4), (7, 2)
UP_OTHER, DOWN_OTHER = UP_OWN, DOWN_OWN


def columns_kernel(
    shells_ref, count_ref, where_ref, screen_ref, mine_ref, other_ref, q_ref, keep_ref, up_ref, down_ref, cw_ref
):
    core = where_ref[0]
    z = where_ref[1]
    way = where_ref[2]
    lane = lax.broadcasted_iota(jnp.int32, (64, 128), 1)

    def weighted(k, want):
        m = shells_ref[0, 0, k]
        n = shells_ref[0, 1, k]
        row = screen_ref[pl.ds(m, 1), :]
        at = lax.broadcasted_iota(jnp.int32, (1, 144), 1) == n
        live = jnp.sum(jnp.where(at, row, 0), axis=1, keepdims=True) == 1
        live = live & (k < count_ref[0, 0])
        a = shell_block(n, z, way, mine_ref, want)
        b = shell_block(n, z, -way, other_ref, want)
        t = jnp.concatenate([jnp.where(core == 0, a, b), jnp.where(core == 0, b, a)], axis=0)
        return jnp.where(live, t, 0.0)

    cols = []
    for k in range(4):
        low, high = weighted(2 * k, 0), weighted(2 * k + 1, 1)
        cols.append(jnp.where(lane < 64, low, high).astype(bf16))
    r = lax.broadcasted_iota(jnp.int32, (256, 1024), 0)
    c = lax.broadcasted_iota(jnp.int32, (256, 1024), 1)
    order = (((r & 63) << 2) + (r >> 6) == ((c >> 4) << 2) + (c & 3)).astype(f32).astype(bf16)
    column = (lax.broadcasted_iota(jnp.int32, (64, 1024), 1) >> 2) & 3
    for half in range(2):
        four = jnp.concatenate(cols[2 * half : 2 * half + 2], axis=1)
        wide = jnp.dot(four, order, preferred_element_type=f32)
        for i in range(4):
            cw_ref[i * 64 : (i + 1) * 64, half * 1024 : (half + 1) * 1024] = jnp.where(
                column == i, wide, 0.0
            ).astype(bf16)
    second_product(z, way, cw_ref, q_ref, keep_ref, (up_ref, UP_OWN), (down_ref, DOWN_OWN))


def own_second(shells, count, where, screen, mine, other, q):
    return pl.pallas_call(
        columns_kernel,
        in_specs=[SMEM] * 3 + [VMEM] * 4,
        out_specs=[VMEM] * 4,
        out_shape=[
            jax.ShapeDtypeStruct((768, 128), f32),
            jax.ShapeDtypeStruct((256 * len(UP_OWN), 128), bf16),
            jax.ShapeDtypeStruct((256 * len(DOWN_OWN), 128), bf16),
            jax.ShapeDtypeStruct((256, 2048), bf16),
        ],
        compiler_params=pltpu.CompilerParams(vmem_limit_bytes=16 * 2**20),
        cost_estimate=pl.CostEstimate(flops=2**31, bytes_accessed=2**20, transcendentals=0),
    )(shells, count, where, screen, mine, other, pltpu.with_memory_space_constraint(q, pltpu.VMEM))


def other_kernel(
    shells_ref, where_ref, other_ref, cw_ref, xa_ref, xb_ref, keep_ref, up_ref, down_ref, lhs_ref, q_ref
):
    z = where_ref[1]
    way = where_ref[2]
    first_product(shells_ref, z, -way, other_ref, xa_ref, xb_ref, lhs_ref, q_ref)
    second_product(z, way, cw_ref, q_ref, keep_ref, (up_ref, UP_OTHER), (down_ref, DOWN_OTHER))


def other_both(shells, where, other, cw, *x):
    return pl.pallas_call(
        other_kernel,
        in_specs=[SMEM] * 2 + [VMEM] * 4,
        out_specs=[VMEM] * 3,
        out_shape=[
            jax.ShapeDtypeStruct((768, 128), f32),
            jax.ShapeDtypeStruct((256 * len(UP_OTHER), 128), bf16),
            jax.ShapeDtypeStruct((256 * len(DOWN_OTHER), 128), bf16),
        ],
        scratch_shapes=[pltpu.VMEM((256, 256), bf16), pltpu.VMEM((16 * 1024, 128), bf16)],
        compiler_params=pltpu.CompilerParams(vmem_limit_bytes=24 * 2**20),
        cost_estimate=pl.CostEstimate(flops=2**33, bytes_accessed=2**20, transcendentals=0),
    )(shells, where, other, cw, *(pltpu.with_memory_space_constraint(t, pltpu.VMEM) for t in x))


def first_round(up, down):
    return swap(up, 1), swap(down, -1)


def second_round(keep, up_ds, from_ahead, down_ds, from_behind):
    total = {0: keep[:256], 3: keep[256:512], 5: keep[512:]}
    for ds, got, step in ((up_ds, from_ahead, 1), (down_ds, from_behind, -1)):
        for k, d in enumerate(ds):
            to = (step - d) % 8
            total[to] = total[to] + got[k * 256 : (k + 1) * 256].astype(f32)
    return total[0], swap(total[3].astype(bf16), 3), swap(total[5].astype(bf16), -3)


def reduced(total, from_ahead, from_behind):
    return total + from_ahead.astype(f32) + from_behind.astype(f32)


def split(x):
    high = x.astype(bf16)
    return high, (x - high.astype(f32)).astype(bf16)


def final_kernel(m_ref, lam_ref, sig_ref, o_ref, low_ref, high_ref):
    h = m_ref[...].reshape(512, 128)
    sig = sig_ref[...].astype(bf16)
    zero = jnp.zeros_like(sig)
    pair = jnp.concatenate([jnp.concatenate([sig, zero], axis=1), jnp.concatenate([zero, sig], axis=1)], axis=0)
    pair = jnp.concatenate([pair, pair], axis=0)
    t = jnp.dot(jnp.concatenate(split(h), axis=1), pair, preferred_element_type=f32)
    low_ref[...] = t[:, :128]
    high_ref[...] = t[:, 128:]
    cols = []
    for q in range(16):
        low = low_ref[pl.ds(q, 32, stride=16), :]
        high = high_ref[pl.ds(q, 32, stride=16), :]
        cols.append(jnp.concatenate(split(jnp.concatenate([low, high], axis=0)), axis=0))
    lam = jnp.concatenate([lam_ref[pl.ds(k, 32, stride=2), :] for k in (0, 1)] * 2, axis=0).astype(bf16)
    res = lax.dot_general(lam, jnp.concatenate(cols, axis=1), (((0,), (0,)), ((), ())), preferred_element_type=f32)
    for q in range(16):
        o_ref[q] = res[:, q * 128 : (q + 1) * 128]


def final(m, lam, sig):
    return pl.pallas_call(
        final_kernel,
        out_shape=jax.ShapeDtypeStruct((16, 128, 128), f32),
        scratch_shapes=[pltpu.VMEM((512, 128), f32)] * 2,
        compiler_params=pltpu.CompilerParams(vmem_limit_bytes=24 * 2**20),
        cost_estimate=pl.CostEstimate(flops=2**28, bytes_accessed=2**21, transcendentals=0),
    )(m, lam, sig)


def on_device(integrals, block_shells, live_counts, significance, occ_coef, lam_coef, sig_coef):
    core = lax.axis_index("pairs") % 2
    z = lax.axis_index(COEF)
    where = jnp.stack([core, z, 1 - 2 * ((z + core) % 2)]).astype(jnp.int32)

    own = lax.dynamic_slice_in_dim(occ_coef.T, core * 32, 32, axis=0)
    own = own.reshape(32, 9, 128).transpose(1, 0, 2).reshape(288, 128)
    own = jnp.concatenate([own, lam_coef, sig_coef], axis=0)
    ahead = swap(own, 3)
    behind = swap(own, -3)
    x = integrals.transpose(1, 2, 3, 0)
    ahead, behind, x_first = lax.optimization_barrier((ahead, behind, relayout(where, x, 0)))
    from_ahead = swap(jnp.concatenate([own, ahead, behind[:SPLIT]], axis=0), 1)
    from_behind = swap(jnp.concatenate([own, behind, ahead[SPLIT:]], axis=0), -1)
    from_ahead, from_behind, x_second = lax.optimization_barrier((from_ahead, from_behind, relayout(where, x, 1)))
    near = 2 * BLOCK
    mine = jnp.concatenate(
        [own, behind, ahead, from_ahead[:near], from_behind[:near], from_ahead[near:], from_behind[near:]], axis=0
    )
    other = lax.ppermute(mine, "pairs", [(i, i ^ 1) for i in range(32)])

    shells = block_shells.transpose(0, 2, 1)
    q, lam, sig = own_first(shells, where, mine, x_first, x_second)
    keep, up, down, cw = own_second(shells, live_counts, where, significance, mine, other, q)
    own_got = first_round(up, down)
    keep_other, up, down = other_both(shells, where, other, cw, x_first, x_second)
    other_got = first_round(up, down)
    own_half = second_round(keep, UP_OWN, own_got[0], DOWN_OWN, own_got[1])
    other_half = second_round(keep_other, UP_OTHER, other_got[0], DOWN_OTHER, other_got[1])
    a = reduced(*own_half)
    b = reduced(*other_half)
    summed = jnp.concatenate([jnp.where(core == 0, a, b), jnp.where(core == 0, b, a)], axis=0)
    moved = lax.all_to_all(summed.reshape(32, 16, 128), "pairs", 0, 0, tiled=True)

    return final(moved, lam, sig)


def solution(mesh):
    fine = Mesh(mesh.devices.reshape(32, 2, 4), ("pairs",) + COEF)
    placed = (
        P("pairs", COEF, None, None),
        P("pairs", COEF, None),
        P("pairs", COEF),
        P(),
        P(COEF, None),
        P(COEF, None),
        P(COEF, None),
    )
    return jax.shard_map(
        on_device,
        mesh=fine,
        in_specs=placed,
        out_specs=P(("pairs",) + COEF, None, None),
        check_vma=False,
    )
```
